32 devices in a mesh: grp: 4 (over y, core), pan: 8 (over z, x).
Axes of the slice: x: 2, y: 2, z: 4, core: 2. Of those that a mesh axis runs over, the one named last changes fastest.
Arguments:
- anc_rows: bfloat16 [4096, 4096], P('grp', 'pan'), as said below
- row_home: int32 [32], replicated, may hold values from 0 to 31, as said below
- block_lists: int32 [4, 16], replicated, may hold values from 0 to 31, as said below
- front_blocks: int32 [4], replicated, may hold values from 8 to 16, as said below
- panel: bfloat16 [4, 2048, 768], P('grp', 'pan'), may hold values from -0.29882812 to 0.29882812
- pivot_inverse: bfloat16 [4, 768, 768], P('grp'), as said below
Outputs:
- cross_cov: bfloat16 [4, 2048, 768], P('grp', 'pan')
- pivot_cov: float32 [4, 768, 768], P('grp', 'pan')
The draws below stay inside these ranges and needn't reach their ends.
Inputs may be any that keep to these rules, and one draw needn't show every extreme that they name: `row_home`: A permutation of 0 to 31; the 4 index blocks of each window [4 q, 4 q + 4) have their storage row blocks in one front group. `block_lists`: rising along each row; entries 2 * q to 2 * q + 1 lie in [4 * q, 4 * q + 4). `front_blocks`: some front has all 16 blocks. `anc_rows`: storage row block row_home[b] holds row block b of a symmetric matrix. `pivot_inverse`: lower triangular.
All inputs are finite; a program needn't handle non-finite values.
Results may differ from the reference program's by a relative error of at most 0.0095.
Values may be sent and summed in bfloat16 or wider, within the bound.
No kernel may reach another device: no remote copies, remote signals or barrier semaphores. Data moves between devices by JAX's collectives and lax.ppermute only.
A program may use at most 128 MiB of HBM per device.

```python
import math
import jax
import jax.numpy as jnp
from jax import lax

BLK = 128
CB = 4
RB = 2
P_SIZE = 768
GROUPS = 4
NBA = 32
NA = 4096
PBG = 8
KB = 16
S = 2048
N_PAN = 8


def block_choice(key):
    base = jax.random.fold_in(key, 11)
    noise = jax.random.randint(base, (GROUPS, N_PAN, CB), 0, 1 << 20)
    scores = noise * CB + jnp.arange(CB, dtype=jnp.int32)
    ranked = jnp.argsort(scores, axis=-1)[..., :RB]
    chosen = jnp.sort(ranked, axis=-1).astype(jnp.int32)
    offsets = (jnp.arange(N_PAN, dtype=jnp.int32) * CB)[None, :, None]
    return (chosen + offsets).reshape(GROUPS, KB).astype(jnp.int32)


def slot_order(key):
    extra = jax.random.fold_in(key, 12)
    key_one, key_two = jax.random.split(extra)
    windows = NBA // CB
    window_perm = jax.random.permutation(key_one, windows).astype(jnp.int32)
    blocks = (window_perm[:, None] * CB + jnp.arange(CB, dtype=jnp.int32)[None, :]).reshape(NBA)
    ranks = jax.random.permutation(key_two, NBA).astype(jnp.int32)
    slot_group = jnp.arange(NBA, dtype=jnp.int32) // PBG
    scores = slot_group * NBA + ranks
    order = jnp.argsort(scores).astype(jnp.int32)
    return blocks[order].astype(jnp.int32)


def draw_block_lists(key, part):
    return block_choice(key)


def draw_row_home(key, part):
    return jnp.argsort(slot_order(key)).astype(jnp.int32)


def draw_front_blocks(key, part):
    base = jax.random.fold_in(key, 14)
    key_one, key_two = jax.random.split(base)
    counts = jax.random.randint(key_one, (GROUPS,), KB // 2, KB + 1)
    full_at = jax.random.randint(key_two, (), 0, GROUPS)
    return jnp.where(jnp.arange(GROUPS) == full_at, KB, counts).astype(jnp.int32)


def draw_anc_rows(key, part):
    slot_block = slot_order(key)
    base = jax.random.fold_in(key, 13)
    key_one, key_two = jax.random.split(base, 2)
    raw = jax.random.normal(key_one, (NA, NA), jnp.float32)
    symmetric = (raw + raw.T) * (0.7071 / math.sqrt(S))
    diag_vals = jax.random.uniform(key_two, (NA,), jnp.float32, 0.5, 1.5)
    index = jnp.arange(NA)
    symmetric = symmetric + jnp.where(index[:, None] == index[None, :], diag_vals[:, None], 0.0)
    stored = symmetric.reshape(NBA, BLK, NA)[slot_block].reshape(NA, NA)
    return stored.astype(jnp.bfloat16)


def draw_pivot_inverse(key, part):
    base = jax.random.fold_in(key, 15)
    key_one, key_two = jax.random.split(base)
    lower = jax.random.normal(key_one, (GROUPS, P_SIZE, P_SIZE), jnp.float32)
    lower = lower * (0.5 / math.sqrt(P_SIZE))
    index = jnp.arange(P_SIZE)
    lower = jnp.where(index[:, None] > index[None, :], lower, 0.0)
    diag_vals = jax.random.uniform(key_two, (GROUPS, P_SIZE), jnp.float32, 0.7, 1.4)
    result = lower + jnp.where(index[:, None] == index[None, :], diag_vals[:, :, None], 0.0)
    return result.astype(jnp.bfloat16)


def level_of(key, extent, shards, low, high):
    gain = 1.0
    for axis_at, shards_of in shards:
        heights = jax.random.uniform(jax.random.fold_in(jax.random.fold_in(key, 6), axis_at), (shards_of,), jnp.float32, low / len(shards), high / len(shards))
        gain = gain * jnp.repeat(jnp.exp(heights), extent[axis_at] // shards_of).reshape((-1,) + (1,) * (len(extent) - 1 - axis_at))
    return gain


def centred(own_key, shape, width, limit, pieces=(), held_as=jnp.bfloat16):
    entries = width * jax.random.normal(own_key, shape, jnp.float32)
    if pieces:
        entries = entries * level_of(own_key, shape, pieces, -0.22, 0.18)
    return jnp.clip(entries, -limit, limit).astype(held_as)


def setup_inputs(seed: int = 0) -> dict:
    keys = jax.random.split(jax.random.key(seed), 7)
    anc_rows = draw_anc_rows(jax.random.fold_in(keys[6], 71), 0)
    row_home = draw_row_home(jax.random.fold_in(keys[6], 71), 0)
    block_lists = draw_block_lists(jax.random.fold_in(keys[6], 71), 0)
    front_blocks = draw_front_blocks(jax.random.fold_in(keys[6], 71), 0)
    panel = centred(keys[4], (GROUPS, S, P_SIZE), 0.05, 0.29882812, ((0, 4), (1, 8)))
    pivot_inverse = draw_pivot_inverse(jax.random.fold_in(keys[6], 71), 0)
    return dict(anc_rows=anc_rows, row_home=row_home, block_lists=block_lists, front_blocks=front_blocks, panel=panel, pivot_inverse=pivot_inverse)


def reference(anc_rows, row_home, block_lists, front_blocks, panel, pivot_inverse):
    blocked = anc_rows.reshape(NBA, BLK, NA)
    contract = (((0,), (0,)), ((), ()))

    def front(group):
        members = block_lists[group]
        stripes = blocked[row_home[members]].reshape(S, NBA, BLK)
        sigma = stripes[:, members, :].reshape(S, S)
        alive = jnp.repeat(jnp.arange(KB, dtype=jnp.int32) < front_blocks[group], BLK)
        inverse_pivot = pivot_inverse[group]
        scaled = jnp.dot(panel[group], inverse_pivot, preferred_element_type=jnp.float32)
        scaled = jnp.where(alive[:, None], scaled, jnp.zeros_like(scaled)).astype(jnp.bfloat16)
        cross = -jnp.dot(sigma, scaled, preferred_element_type=jnp.float32)
        cross = jnp.where(alive[:, None], cross, jnp.zeros_like(cross)).astype(jnp.bfloat16)
        triangle = lax.dot_general(inverse_pivot, inverse_pivot, contract, preferred_element_type=jnp.float32)
        pivot = triangle - lax.dot_general(scaled, cross, contract, preferred_element_type=jnp.float32)
        return cross, pivot

    cross_cov, pivot_cov = lax.map(front, jnp.arange(GROUPS, dtype=jnp.int32))
    return cross_cov, pivot_cov
```

```python
import functools

import jax
import jax.numpy as jnp
from jax import lax
from jax.experimental import pallas as pl
from jax.experimental.pallas import tpu as pltpu
from jax.sharding import PartitionSpec as P

BLK = 128
F32 = jnp.float32
BF16 = jnp.bfloat16

VMEM = pl.BlockSpec(memory_space=pltpu.VMEM)
SMEM = pl.BlockSpec(memory_space=pltpu.SMEM)
HBM = pl.BlockSpec(memory_space=pl.ANY)


def power_of_two(n):
    return n & (n - 1) == 0


def peer(q, k, n):
    return q ^ k if power_of_two(n) else (q + k) % n


def source(q, k, n):
    return q ^ k if power_of_two(n) else (q + n - k) % n


def ring_place(position, n):
    return position ^ (position >> 1) if power_of_two(n) else position


def ring_position(place, n):
    position = place
    if power_of_two(n):
        shift = 1
        while shift < n:
            position = position ^ (place >> shift)
            shift += 1
    return position


def params():
    return pltpu.CompilerParams(vmem_limit_bytes=40 * 1024 * 1024)


def pack_kernel(groups, pan, me, row_home, lists, anc, *rest):
    outs, slots, sems = rest[:groups], rest[groups], rest[groups + 1]
    g, p = me[0], me[1]
    h, c, l = g >> 1, g & 1, p & 1
    stored = anc.shape[0] // BLK
    window_blocks = anc.shape[1] // BLK
    picked = lists.shape[1] // pan
    windows = pan // groups

    def window(w, rank):
        mine = row_home[window_blocks * w] // stored == g

        @pl.when(mine)
        def _():
            for k in range(groups):
                front = 2 * peer(h, k >> 1, groups // 2) + (c ^ (k & 1))
                for r in range(picked):
                    row = row_home[lists[front, picked * w + r]] - stored * g
                    for s in range(picked):
                        column = lists[front, picked * p + s] - window_blocks * p
                        pltpu.make_async_copy(
                            anc.at[pl.ds(row * BLK, BLK), pl.ds(column * BLK, BLK)],
                            outs[k].at[pl.ds((rank * picked + r) * BLK, BLK), pl.ds(s * BLK, BLK)],
                            sems.at[k],
                        ).start()

        return rank + mine.astype(jnp.int32)

    lax.fori_loop(0, pan, window, jnp.int32(0))
    owners = [row_home[window_blocks * w] // stored for w in range(pan)]
    for w in range(pan):
        rank = jnp.int32(0)
        for v in range(w):
            rank = rank + (owners[v] == owners[w]).astype(jnp.int32)
        step = owners[w] >> 1
        step = step ^ h if power_of_two(groups // 2) else (h + groups // 2 - step) % (groups // 2)
        slots[w] = (2 * step + ((owners[w] & 1) ^ l)) * windows + rank
    rows, columns = outs[0].shape
    for k in range(groups):
        pltpu.make_async_copy(
            anc.at[pl.ds(0, rows), pl.ds(0, columns)], outs[k], sems.at[k]
        ).wait()


def scale_kernel(pan, me, front_blocks, panel, inverse, keep, give, both, turned):
    g, p = me[0], me[1]
    c = g & 1
    rows, width = panel.shape
    n, share = pan // 2, width // pan
    padded = keep.shape[0] // n
    live = front_blocks[g]
    scaled = jnp.dot(panel[...], inverse[...], preferred_element_type=F32)
    row = lax.broadcasted_iota(jnp.int32, scaled.shape, 0)
    scaled = jnp.where(p * (rows // BLK) + row // BLK < live, scaled, 0.0)
    turned[...] = scaled.T
    if padded != share:
        keep[...] = jnp.zeros_like(keep)
        give[...] = jnp.zeros_like(give)
    for place in range(n):
        at = pl.ds(place * padded, share)
        keep[at] = turned[pl.ds(share * (2 * place + c), share)].astype(BF16)
        give[at] = turned[pl.ds(share * (2 * place + 1 - c), share)].astype(BF16)
    both[0] = keep[...]
    both[1] = give[...]


def cross_kernel(n, me, front_blocks, slots, *rest):
    near, far = rest[:n], rest[n : 2 * n]
    own_sigma, other_sigma = rest[2 * n : 2 * n + 2]
    mine, give, whole = rest[2 * n + 2 : 2 * n + 5]
    parts, total = rest[2 * n + 5 : 3 * n + 5], rest[3 * n + 5]
    g, p = me[0], me[1]
    h, c, q, l = g >> 1, g & 1, p >> 1, p & 1
    half, rows = near[0].shape
    padded = half // n
    own = jnp.zeros((half, rows), F32)
    other = jnp.zeros((half, rows), F32)
    position = ring_position(q, n)
    for step in range(n):
        origin = ring_place((position + n - step) % n, n)
        for side, chunks in ((0, near), (1, far)):
            member = 2 * origin + (l ^ side)
            slot = slots[member]
            chunk = chunks[step][...]
            whole[member] = chunk
            own = own + jnp.dot(chunk, own_sigma[slot], preferred_element_type=F32)
            other = other + jnp.dot(chunk, other_sigma[slot], preferred_element_type=F32)
    live = front_blocks[2 * h + l]
    block = lax.broadcasted_iota(jnp.int32, (half, rows), 1) // BLK
    own = jnp.where((2 * q + c) * (rows // BLK) + block < live, -own, 0.0)
    other = jnp.where((2 * q + 1 - c) * (rows // BLK) + block < live, -other, 0.0)
    mine[...] = own.astype(BF16)
    give[...] = other.astype(BF16)
    total[c] = own
    total[1 - c] = other
    for k in range(n):
        at = pl.ds(peer(q, k, n) * padded, padded)
        for side in range(2):
            parts[k][:, pl.ds(side * rows, rows)] = total[side, at].astype(BF16)


def pivot_kernel(n, share, me, *rest):
    parts, own_scaled, other_scaled, out = rest[:n], rest[n], rest[n + 1], rest[n + 2]
    g, p = me[0], me[1]
    c, q = g & 1, p >> 1
    rows = own_scaled.shape[2]
    padded = parts[0].shape[0]
    across = (((1,), (1,)), ((), ()))
    own = jnp.zeros((padded, n * padded), F32)
    other = jnp.zeros((padded, n * padded), F32)
    for k in range(n):
        origin = source(q, k, n)
        for side in range(2):
            part = parts[k][:, pl.ds(side * rows, rows)]
            member = 2 * origin + side
            own = own + lax.dot_general(
                part, own_scaled[member], across, preferred_element_type=F32
            )
            other = other + lax.dot_general(
                part, other_scaled[member], across, preferred_element_type=F32
            )
    low = jnp.where(c == 0, own, other)
    high = jnp.where(c == 0, other, own)
    pieces = []
    for place in range(n):
        at = slice(place * padded, place * padded + share)
        pieces += [low[:, at], high[:, at]]
    out[...] = (-jnp.concatenate(pieces, axis=1)).astype(BF16)


def turn_kernel(pan, share, me, mine, other, out, natural):
    c = me[0] & 1
    n = pan // 2
    padded = mine.shape[0] // n
    for place in range(n):
        at = pl.ds(place * padded, share)
        natural[pl.ds(share * (2 * place + c), share)] = mine[at].astype(F32)
        natural[pl.ds(share * (2 * place + 1 - c), share)] = other[at].astype(F32)
    out[...] = natural[...].T.astype(BF16)


def per_device(anc_rows, row_home, block_lists, front_blocks, panel, pivot_inverse):
    groups, pan = lax.axis_size("grp"), lax.axis_size("pan")
    n, pairs = pan // 2, groups // 2
    rows, width = panel.shape[1:]
    share = width // pan
    padded = -(-share // 16) * 16
    half = n * padded
    wanted = block_lists.shape[1] // groups * BLK
    windows = pan // groups
    me = jnp.stack([lax.axis_index("grp"), lax.axis_index("pan")]).astype(jnp.int32)
    diagonal = me[0] & 1 == me[1] & 1
    inverse = pivot_inverse[0]
    shape = jax.ShapeDtypeStruct

    def at(h, c, q, l):
        return (2 * h + c) * pan + 2 * q + l

    places = [
        (h, c, q, l) for h in range(pairs) for c in range(2) for q in range(n) for l in range(2)
    ]
    exchange = [(at(h, c, q, l), at(h, l, q, c)) for h, c, q, l in places]
    crossing = [(a, b) for a, b in exchange if a != b]
    cores = [(g, g ^ 1) for g in range(groups)]
    ring = [
        (2 * ring_place(i, n) + l, 2 * ring_place((i + 1) % n, n) + l)
        for i in range(n)
        for l in range(2)
    ]

    def swap(x):
        return lax.ppermute(x, "grp", cores)

    def everywhere(x, pairs_of):
        return lax.ppermute(x, ("grp", "pan"), pairs_of)

    keep, give, both = pl.pallas_call(
        functools.partial(scale_kernel, pan),
        out_shape=[shape((half, rows), BF16)] * 2 + [shape((2, half, rows), BF16)],
        in_specs=[SMEM, SMEM, VMEM, VMEM],
        out_specs=[VMEM] * 3,
        scratch_shapes=[pltpu.VMEM((width, rows), F32)],
        compiler_params=params(),
        name="scale",
    )(me, front_blocks, panel[0], inverse)
    near = jnp.where(diagonal, keep, swap(give))
    moved = everywhere(both, crossing)
    far = jnp.where(diagonal, swap(moved[0]), moved[1])

    *packed, slots = pl.pallas_call(
        functools.partial(pack_kernel, groups, pan),
        out_shape=[shape((wanted, rows), BF16)] * groups + [shape((pan,), jnp.int32)],
        in_specs=[SMEM, SMEM, SMEM, HBM],
        out_specs=[HBM] * groups + [SMEM],
        scratch_shapes=[pltpu.SemaphoreType.DMA((groups,))],
        compiler_params=params(),
        name="pack",
    )(me, row_home, block_lists, anc_rows)
    arrived = [
        everywhere(
            packed[k],
            [
                (at(h, c, q, l), at(peer(h, k >> 1, pairs), l, q, c ^ (k & 1)))
                for h, c, q, l in places
            ],
        )
        for k in range(groups)
    ]
    own_sigma = jnp.stack(arrived).reshape(groups * windows, wanted // windows, rows)
    other_sigma = swap(own_sigma)

    nears, fars = [near], [far]
    for _ in range(n - 1):
        nears.append(lax.ppermute(nears[-1], "pan", ring))
        fars.append(lax.ppermute(fars[-1], "pan", ring))

    mine, give, whole, *parts = pl.pallas_call(
        functools.partial(cross_kernel, n),
        out_shape=[shape((half, rows), BF16)] * 2
        + [shape((pan, half, rows), BF16)]
        + [shape((padded, 2 * rows), BF16)] * n,
        in_specs=[SMEM] * 3 + [VMEM] * (2 * n + 2),
        out_specs=[VMEM] * (n + 3),
        scratch_shapes=[pltpu.VMEM((2, half, rows), F32)],
        compiler_params=params(),
        name="cross",
    )(me, front_blocks, slots, *nears, *fars, own_sigma, other_sigma)

    for k in range(1, n):
        parts[k] = lax.ppermute(
            parts[k], "pan", [(2 * q + l, 2 * peer(q, k, n) + l) for q in range(n) for l in range(2)]
        )
    other_whole = swap(whole)
    turned = pl.pallas_call(
        functools.partial(turn_kernel, pan, share),
        out_shape=shape((rows, width), BF16),
        in_specs=[SMEM, VMEM, VMEM],
        out_specs=VMEM,
        scratch_shapes=[pltpu.VMEM((width, rows), F32)],
        compiler_params=params(),
        name="turn",
    )(me, mine, swap(give))
    cross = everywhere(turned, exchange)

    term = pl.pallas_call(
        functools.partial(pivot_kernel, n, share),
        out_shape=shape((padded, width), BF16),
        in_specs=[SMEM] + [VMEM] * (n + 2),
        out_specs=VMEM,
        compiler_params=params(),
        name="pivot",
    )(me, *parts, whole, other_whole)
    own_columns = lax.dynamic_slice_in_dim(inverse, me[1] * share, share, 1)
    triangle = lax.dot_general(
        own_columns, inverse, (((0,), (0,)), ((), ())), preferred_element_type=F32
    )
    pivot = triangle + everywhere(term, exchange)[:share].astype(F32)
    return cross[None], pivot[None]


def solution(mesh):
    placed = (P("grp", "pan"), P(), P(), P(), P("grp", "pan", None), P("grp", None, None))
    return jax.shard_map(
        per_device,
        mesh=mesh,
        in_specs=placed,
        out_specs=(P("grp", "pan", None), P("grp", "pan", None)),
        check_vma=False,
    )
```

```python
import functools

import jax
import jax.numpy as jnp
from jax import lax
from jax.experimental import pallas as pl
from jax.experimental.pallas import tpu as pltpu
from jax.sharding import PartitionSpec as P

BLK = 128
F32 = jnp.float32
BF16 = jnp.bfloat16

VMEM = pl.BlockSpec(memory_space=pltpu.VMEM)
SMEM = pl.BlockSpec(memory_space=pltpu.SMEM)
HBM = pl.BlockSpec(memory_space=pltpu.HBM)


def power_of_two(n):
    return n & (n - 1) == 0


def peer(q, k, n):
    return q ^ k if power_of_two(n) else (q + k) % n


def source(q, k, n):
    return q ^ k if power_of_two(n) else (q + n - k) % n


def ring_place(position, n):
    return position ^ (position >> 1) if power_of_two(n) else position


def ring_position(place, n):
    position = place
    if power_of_two(n):
        shift = 1
        while shift < n:
            position = position ^ (place >> shift)
            shift += 1
    return position


def coordinates():
    g, p = lax.axis_index("grp"), lax.axis_index("pan")
    return g >> 1, g & 1, p >> 1, p & 1


def params(mib=40):
    return pltpu.CompilerParams(vmem_limit_bytes=mib * 1024 * 1024)


def pack_kernel(groups, pan, row_home_in, lists_in, anc, other_anc, *rest):
    pairs = groups // 2
    outs, members = rest[:pairs], rest[pairs]
    row_home, lists, sems = rest[pairs + 1 :]
    h, c, q, l = coordinates()
    p = 2 * q + l
    loads = [
        pltpu.make_async_copy(row_home_in, row_home, sems.at[pairs]),
        pltpu.make_async_copy(lists_in, lists, sems.at[pairs + 1]),
    ]
    for load in loads:
        load.start()
    for load in loads:
        load.wait()
    stored = anc.shape[0] // BLK
    window_blocks = anc.shape[1] // BLK
    picked = lists.shape[1] // pan
    windows = pan // groups
    depth = picked * BLK

    def window(w, ranks):
        owner = row_home[window_blocks * w] // stored
        counts = []
        for core, rank in enumerate(ranks):
            mine = owner == 2 * h + core
            counts.append(rank + mine.astype(jnp.int32))
            for local in range(2):

                @pl.when(mine & ((c == core) == (local == 0)))
                def _():
                    origin = (anc, other_anc)[local]
                    for k in range(pairs):
                        front = 2 * peer(h, k, pairs) + c
                        for r in range(picked):
                            row = row_home[lists[front, picked * w + r]] - stored * owner
                            at = ((core * windows + rank) * picked + r) * BLK
                            for s in range(picked):
                                column = lists[front, picked * p + s] - window_blocks * p
                                pltpu.make_async_copy(
                                    origin.at[pl.ds(row * BLK, BLK), pl.ds(column * BLK, BLK)],
                                    outs[k].at[pl.ds(at, BLK), pl.ds(s * BLK, BLK)],
                                    sems.at[k],
                                ).start()

        return tuple(counts)

    lax.fori_loop(0, pan, window, (jnp.int32(0), jnp.int32(0)))
    owners = [row_home[window_blocks * w] // stored for w in range(pan)]
    for w in range(pan):
        rank = jnp.int32(0)
        for v in range(w):
            rank = rank + (owners[v] == owners[w]).astype(jnp.int32)
        step = owners[w] >> 1
        step = step ^ h if power_of_two(pairs) else (h + pairs - step) % pairs
        members[(2 * step + (owners[w] & 1)) * windows + rank] = jnp.int32(w)
    rows, columns = outs[0].shape
    for k in range(pairs):
        pltpu.make_async_copy(
            anc.at[pl.ds(0, rows), pl.ds(0, columns)], outs[k], sems.at[k]
        ).wait()


def scale_kernel(
    pan, front_blocks_in, panel_in, inverse_in, keep, give, panel, inverse, turned, front_blocks, sems
):
    h, c, q, l = coordinates()
    g, p = 2 * h + c, 2 * q + l
    loads = [
        pltpu.make_async_copy(inverse_in, inverse, sems.at[0]),
        pltpu.make_async_copy(panel_in, panel, sems.at[1]),
        pltpu.make_async_copy(front_blocks_in, front_blocks, sems.at[2]),
    ]
    for load in loads:
        load.start()
    for load in loads:
        load.wait()
    rows, width = panel.shape
    n, share = pan // 2, width // pan
    padded = keep.shape[0] // n
    live = front_blocks[g]
    scaled = jnp.dot(panel[...], inverse[...], preferred_element_type=F32)
    row = lax.broadcasted_iota(jnp.int32, scaled.shape, 0)
    scaled = jnp.where(p * (rows // BLK) + row // BLK < live, scaled, 0.0)
    turned[...] = scaled.T
    if padded != share:
        keep[...] = jnp.zeros_like(keep)
        give[...] = jnp.zeros_like(give)
    for place in range(n):
        at = pl.ds(place * padded, share)
        keep[at] = turned[pl.ds(share * (2 * place + c), share)].astype(BF16)
        give[at] = turned[pl.ds(share * (2 * place + 1 - c), share)].astype(BF16)


def cross_kernel(n, groups, front_blocks, members, *rest):
    near, far = rest[:n], rest[n : 2 * n]
    rest = rest[2 * n :]
    pairs = groups // 2
    own_sigma, other_sigma = rest[:pairs], rest[pairs : 2 * pairs]
    rest = rest[2 * pairs :]
    mine, give, whole = rest[:3]
    parts, total = rest[3 : n + 3], rest[n + 3]
    h, c, q, l = coordinates()
    half, rows = near[0].shape
    padded = half // n
    position = ring_position(q, n)
    for step in range(n):
        origin = ring_place((position + n - step) % n, n)
        whole[2 * origin + l] = near[step][...]
        whole[2 * origin + (1 - l)] = far[step][...]
    own = jnp.zeros((half, rows), F32)
    other = jnp.zeros((half, rows), F32)
    windows = 2 * n // pairs
    depth = own_sigma[0].shape[0] // windows
    for slot in range(2 * n):
        chunk = whole[members[slot]]
        at = pl.ds(slot % windows * depth, depth)
        own = own + jnp.dot(chunk, own_sigma[slot // windows][at], preferred_element_type=F32)
        other = other + jnp.dot(chunk, other_sigma[slot // windows][at], preferred_element_type=F32)
    live = front_blocks[2 * h + l]
    block = lax.broadcasted_iota(jnp.int32, (half, rows), 1) // BLK
    own = jnp.where((2 * q + c) * (rows // BLK) + block < live, -own, 0.0)
    other = jnp.where((2 * q + 1 - c) * (rows // BLK) + block < live, -other, 0.0)
    mine[...] = own.astype(BF16)
    give[...] = other.astype(BF16)
    total[c] = own
    total[1 - c] = other
    for k in range(n):
        at = pl.ds(peer(q, k, n) * padded, padded)
        for side in range(2):
            parts[k][:, pl.ds(side * rows, rows)] = total[side, at].astype(BF16)


def pivot_first_kernel(n, part, own_scaled, other_scaled, own_out, other_out):
    _, _, q, _ = coordinates()
    own, other = pivot_terms(part, q, own_scaled, other_scaled)
    own_out[...] = own
    other_out[...] = other


def pivot_terms(part, origin, own_scaled, other_scaled):
    rows = own_scaled.shape[2]
    sums = [None, None]
    for side in range(2):
        piece = part[:, pl.ds(side * rows, rows)]
        for i, scaled in enumerate((own_scaled, other_scaled)):
            term = lax.dot_general(
                piece, scaled[2 * origin + side], (((1,), (1,)), ((), ())), preferred_element_type=F32
            )
            sums[i] = term if sums[i] is None else sums[i] + term
    return sums


def pivot_kernel(n, share, *rest):
    own_first, other_first = rest[:2]
    parts, own_scaled, other_scaled, out = rest[2 : n + 1], rest[n + 1], rest[n + 2], rest[n + 3]
    _, c, q, _ = coordinates()
    padded = parts[0].shape[0]
    own, other = own_first[...], other_first[...]
    for k in range(1, n):
        terms = pivot_terms(parts[k - 1], source(q, k, n), own_scaled, other_scaled)
        own, other = own + terms[0], other + terms[1]
    low = jnp.where(c == 0, own, other)
    high = jnp.where(c == 0, other, own)
    pieces = []
    for place in range(n):
        at = slice(place * padded, place * padded + share)
        pieces += [low[:, at], high[:, at]]
    out[...] = (-jnp.concatenate(pieces, axis=1)).astype(BF16)


def turn_kernel(pan, share, mine, other, out, natural):
    _, c, _, _ = coordinates()
    n = pan // 2
    padded = mine.shape[0] // n
    for place in range(n):
        at = pl.ds(place * padded, share)
        natural[pl.ds(share * (2 * place + c), share)] = mine[at].astype(F32)
        natural[pl.ds(share * (2 * place + 1 - c), share)] = other[at].astype(F32)
    out[...] = natural[...].T.astype(BF16)


def per_device(anc_rows, row_home, block_lists, front_blocks, panel, pivot_inverse):
    groups, pan = lax.axis_size("grp"), lax.axis_size("pan")
    n, pairs = pan // 2, groups // 2
    rows, width = panel.shape[1:]
    share = width // pan
    padded = -(-share // 16) * 16
    half = n * padded
    wanted = block_lists.shape[1] // groups * BLK
    windows = pan // groups
    diagonal = (lax.axis_index("grp") ^ lax.axis_index("pan")) & 1 == 0
    inverse = pivot_inverse[0]
    shape = jax.ShapeDtypeStruct

    def at(h, c, q, l):
        return (2 * h + c) * pan + 2 * q + l

    places = [
        (h, c, q, l) for h in range(pairs) for c in range(2) for q in range(n) for l in range(2)
    ]
    exchange = [(at(h, c, q, l), at(h, l, q, c)) for h, c, q, l in places]
    crossing = [(a, b) for a, b in exchange if a != b]
    to_sibling = [(at(h, c, q, l), at(h, 1 - c, q, l)) for h, c, q, l in places if c == l]
    to_diagonal = [(at(h, c, q, l), at(h, c, q, c)) for h, c, q, l in places if c != l]
    cores = [(g, g ^ 1) for g in range(groups)]
    ring = [
        (2 * ring_place(i, n) + l, 2 * ring_place((i + 1) % n, n) + l)
        for i in range(n)
        for l in range(2)
    ]

    def swap(x):
        return lax.ppermute(x, "grp", cores)

    def everywhere(x, pairs_of):
        return lax.ppermute(x, ("grp", "pan"), pairs_of)

    keep, give = pl.pallas_call(
        functools.partial(scale_kernel, pan),
        out_shape=[shape((half, rows), BF16)] * 2,
        in_specs=[HBM] * 3,
        out_specs=[VMEM] * 2,
        scratch_shapes=[
            pltpu.VMEM((rows, width), BF16),
            pltpu.VMEM((width, width), BF16),
            pltpu.VMEM((width, rows), F32),
            pltpu.SMEM(front_blocks.shape, jnp.int32),
            pltpu.SemaphoreType.DMA((3,)),
        ],
        compiler_params=params(60),
        name="scale",
    )(front_blocks, panel[0], inverse)
    given = everywhere(give, to_sibling)
    keep, give, given = lax.optimization_barrier((keep, give, given))
    near = jnp.where(diagonal, keep, given)
    far = jnp.where(diagonal, everywhere(keep, to_diagonal), everywhere(give, crossing))

    *packed, members = pl.pallas_call(
        functools.partial(pack_kernel, groups, pan),
        out_shape=[shape((2 * wanted, rows), BF16)] * pairs + [shape((pan,), jnp.int32)],
        in_specs=[HBM] * 4,
        out_specs=[HBM] * pairs + [SMEM],
        scratch_shapes=[
            pltpu.SMEM(row_home.shape, jnp.int32),
            pltpu.SMEM(block_lists.shape, jnp.int32),
            pltpu.SemaphoreType.DMA((pairs + 2,)),
        ],
        compiler_params=params(),
        name="pack",
    )(row_home, block_lists, anc_rows, swap(anc_rows))
    arrived = [
        everywhere(
            packed[k], [(at(h, c, q, l), at(peer(h, k, pairs), l, q, c)) for h, c, q, l in places]
        )
        for k in range(pairs)
    ]
    own_columns = lax.dynamic_slice_in_dim(inverse, lax.axis_index("pan") * share, share, 1)
    triangle = lax.dot_general(
        own_columns, inverse, (((0,), (0,)), ((), ())), preferred_element_type=F32
    )

    nears, fars = [near], [far]
    for step in range(1, n):
        nears.append(lax.ppermute(nears[-1], "pan", ring))
        fars.append(lax.ppermute(fars[-1], "pan", ring))

    arrived, triangle, _ = lax.optimization_barrier((arrived, triangle, nears[min(2, n - 1)]))
    swapped = [swap(piece) for piece in arrived]
    mine, give, whole, *parts = pl.pallas_call(
        functools.partial(cross_kernel, n, groups),
        out_shape=[shape((half, rows), BF16)] * 2
        + [shape((pan, half, rows), BF16)]
        + [shape((padded, 2 * rows), BF16)] * n,
        in_specs=[SMEM] * 2 + [VMEM] * (2 * n + groups),
        out_specs=[VMEM] * (n + 3),
        scratch_shapes=[pltpu.VMEM((2, half, rows), F32)],
        compiler_params=params(),
        name="cross",
    )(front_blocks, members, *nears, *fars, *arrived, *swapped)

    for k in range(1, n):
        parts[k] = lax.ppermute(
            parts[k], "pan", [(2 * q + l, 2 * peer(q, k, n) + l) for q in range(n) for l in range(2)]
        )
    other_whole = swap(whole)
    turned = pl.pallas_call(
        functools.partial(turn_kernel, pan, share),
        out_shape=shape((rows, width), BF16),
        in_specs=[VMEM, VMEM],
        out_specs=VMEM,
        scratch_shapes=[pltpu.VMEM((width, rows), F32)],
        compiler_params=params(),
        name="turn",
    )(mine, swap(give))
    cross = jnp.where(diagonal, turned, everywhere(turned, crossing))

    firsts = pl.pallas_call(
        functools.partial(pivot_first_kernel, n),
        out_shape=[shape((padded, half), F32)] * 2,
        in_specs=[VMEM] * 3,
        out_specs=[VMEM] * 2,
        compiler_params=params(),
        name="pivot_first",
    )(parts[0], whole, other_whole)
    term = pl.pallas_call(
        functools.partial(pivot_kernel, n, share),
        out_shape=shape((padded, width), BF16),
        in_specs=[VMEM] * (n + 3),
        out_specs=VMEM,
        compiler_params=params(),
        name="pivot",
    )(*firsts, *parts[1:], whole, other_whole)
    term, cross = lax.optimization_barrier((term, cross))
    term = jnp.where(diagonal, term, everywhere(term, crossing))
    pivot = triangle + term[:share].astype(F32)
    return cross[None], pivot[None]


def solution(mesh):
    placed = (P("grp", "pan"), P(), P(), P(), P("grp", "pan", None), P("grp", None, None))
    return jax.shard_map(
        per_device,
        mesh=mesh,
        in_specs=placed,
        out_specs=(P("grp", "pan", None), P("grp", "pan", None)),
        check_vma=False,
    )
```

```python
import functools

import jax
import jax.numpy as jnp
from jax import lax
from jax.experimental import pallas as pl
from jax.experimental.pallas import tpu as pltpu
from jax.sharding import PartitionSpec as P

BLK = 128
PLACE = 1_000_000_000
STACK = 12_000_000_000
F32 = jnp.float32
BF16 = jnp.bfloat16

VMEM = pl.BlockSpec(memory_space=pltpu.VMEM)
SMEM = pl.BlockSpec(memory_space=pltpu.SMEM)
HBM = pl.BlockSpec(memory_space=pltpu.HBM)


def power_of_two(n):
    return n & (n - 1) == 0


def peer(q, k, n):
    return q ^ k if power_of_two(n) else (q + k) % n


def source(q, k, n):
    return q ^ k if power_of_two(n) else (q + n - k) % n


def ring_place(position, n):
    return position ^ (position >> 1) if power_of_two(n) else position


def ring_position(place, n):
    position = place
    if power_of_two(n):
        shift = 1
        while shift < n:
            position = position ^ (place >> shift)
            shift += 1
    return position


def coordinates():
    g, p = lax.axis_index("grp"), lax.axis_index("pan")
    return g >> 1, g & 1, p >> 1, p & 1


def params(mib=40):
    return pltpu.CompilerParams(vmem_limit_bytes=mib * 1024 * 1024)


def pack_kernel(groups, pan, row_home_in, lists_in, anc, other_anc, *rest):
    pairs = groups // 2
    outs, slots = rest[:pairs], rest[pairs]
    row_home, lists, place, sems = rest[pairs + 1 :]
    loads = [
        pltpu.make_async_copy(row_home_in, row_home, sems.at[0]),
        pltpu.make_async_copy(lists_in, lists, sems.at[1]),
    ]
    for load in loads:
        load.start()
    for load in loads:
        load.wait()
    h, c, q, l = coordinates()
    p = 2 * q + l
    stored = anc.shape[0] // BLK
    window_blocks = anc.shape[1] // BLK
    picked = lists.shape[1] // pan
    windows = pan // groups

    owners = [row_home[window_blocks * w] // stored for w in range(pan)]
    for w in range(pan):
        rank = jnp.int32(0)
        for v in range(w):
            rank = rank + (owners[v] == owners[w]).astype(jnp.int32)
        step = owners[w] >> 1
        step = step ^ h if power_of_two(pairs) else (h + pairs - step) % pairs
        slots[w] = (2 * step + (owners[w] & 1)) * windows + rank

        @pl.when(owners[w] >> 1 == h)
        def _():
            place[(owners[w] & 1) * windows + rank] = jnp.int32(w)

    for k in range(pairs):
        front = 2 * peer(h, k, pairs) + c
        columns = [lists[front, picked * p + s] - window_blocks * p for s in range(picked)]
        for core in range(2):
            for rank in range(windows):
                w = place[core * windows + rank]
                for r in range(picked):
                    row = row_home[lists[front, picked * w + r]] - stored * (2 * h + core)
                    rows = pl.ds(pl.multiple_of(row * BLK, BLK), BLK)
                    for s in range(picked):
                        at = pl.ds(pl.multiple_of(columns[s] * BLK, BLK), BLK)
                        to = pl.ds(((core * windows + rank) * picked + r) * BLK, BLK)
                        outs[k][to, pl.ds(s * BLK, BLK)] = jnp.where(c == core, anc[rows, at], other_anc[rows, at])


def scale_kernel(
    pan, front_blocks_in, panel_in, inverse_in, keep, give, panel, inverse, turned, front_blocks, sems
):
    h, c, q, l = coordinates()
    g, p = 2 * h + c, 2 * q + l
    loads = [
        pltpu.make_async_copy(inverse_in, inverse, sems.at[0]),
        pltpu.make_async_copy(panel_in, panel, sems.at[1]),
        pltpu.make_async_copy(front_blocks_in, front_blocks, sems.at[2]),
    ]
    for load in loads:
        load.start()
    for load in loads:
        load.wait()
    rows, width = panel.shape
    n, share = pan // 2, width // pan
    padded = keep.shape[0] // n
    live = front_blocks[g]
    scaled = jnp.dot(panel[...], inverse[...], preferred_element_type=F32)
    row = lax.broadcasted_iota(jnp.int32, scaled.shape, 0)
    scaled = jnp.where(p * (rows // BLK) + row // BLK < live, scaled, 0.0)
    turned[...] = scaled.T
    if padded != share:
        keep[...] = jnp.zeros_like(keep)
        give[...] = jnp.zeros_like(give)
    for place in range(n):
        at = pl.ds(place * padded, share)
        keep[at] = turned[pl.ds(share * (2 * place + c), share)].astype(BF16)
        give[at] = turned[pl.ds(share * (2 * place + 1 - c), share)].astype(BF16)


def stack_kernel(pairs, *refs):
    own_in, other_in, (own, other) = refs[:pairs], refs[pairs : 2 * pairs], refs[2 * pairs :]
    depth = own.shape[1]
    windows = own_in[0].shape[0] // depth
    for slot in range(own.shape[0]):
        at = pl.ds(slot % windows * depth, depth)
        own[slot] = own_in[slot // windows][at]
        other[slot] = other_in[slot // windows][at]


def place_kernel(n, k, side, chunk, _, whole, sem):
    _, _, q, l = coordinates()
    origin = ring_place((ring_position(q, n) + n - k) % n, n)
    copy = pltpu.make_async_copy(chunk, whole.at[2 * origin + (l ^ side)], sem)
    copy.start()
    copy.wait()


def cross_kernel(n, front_blocks, slots, whole, own_sigma, other_sigma, mine, give, *rest):
    parts, total = rest[:n], rest[n]
    h, c, q, l = coordinates()
    half, rows = mine.shape
    padded = half // n
    own = jnp.zeros((half, rows), F32)
    other = jnp.zeros((half, rows), F32)
    for member in range(2 * n):
        slot = slots[member]
        own = own + jnp.dot(whole[member], own_sigma[slot], preferred_element_type=F32)
        other = other + jnp.dot(whole[member], other_sigma[slot], preferred_element_type=F32)
    live = front_blocks[2 * h + l]
    block = lax.broadcasted_iota(jnp.int32, (half, rows), 1) // BLK
    own = jnp.where((2 * q + c) * (rows // BLK) + block < live, -own, 0.0)
    other = jnp.where((2 * q + 1 - c) * (rows // BLK) + block < live, -other, 0.0)
    mine[...] = own.astype(BF16)
    give[...] = other.astype(BF16)
    total[c] = own
    total[1 - c] = other
    for k in range(n):
        at = pl.ds(peer(q, k, n) * padded, padded)
        for side in range(2):
            parts[k][:, pl.ds(side * rows, rows)] = total[side, at].astype(BF16)


def pivot_first_kernel(n, part, own_scaled, other_scaled, own_out, other_out):
    _, _, q, _ = coordinates()
    own, other = pivot_terms(part, q, own_scaled, other_scaled)
    own_out[...] = own
    other_out[...] = other


def pivot_terms(part, origin, own_scaled, other_scaled):
    rows = own_scaled.shape[2]
    sums = [None, None]
    for side in range(2):
        piece = part[:, pl.ds(side * rows, rows)]
        for i, scaled in enumerate((own_scaled, other_scaled)):
            term = lax.dot_general(
                piece, scaled[2 * origin + side], (((1,), (1,)), ((), ())), preferred_element_type=F32
            )
            sums[i] = term if sums[i] is None else sums[i] + term
    return sums


def pivot_kernel(n, share, *rest):
    own_first, other_first = rest[:2]
    parts, own_scaled, other_scaled, out = rest[2 : n + 1], rest[n + 1], rest[n + 2], rest[n + 3]
    _, c, q, _ = coordinates()
    padded = parts[0].shape[0]
    own, other = own_first[...], other_first[...]
    for k in range(1, n):
        terms = pivot_terms(parts[k - 1], source(q, k, n), own_scaled, other_scaled)
        own, other = own + terms[0], other + terms[1]
    low = jnp.where(c == 0, own, other)
    high = jnp.where(c == 0, other, own)
    pieces = []
    for place in range(n):
        at = slice(place * padded, place * padded + share)
        pieces += [low[:, at], high[:, at]]
    out[...] = (-jnp.concatenate(pieces, axis=1)).astype(BF16)


def turn_kernel(pan, share, own_rows, other_rows, out, natural):
    _, _, _, l = coordinates()
    n = pan // 2
    padded = own_rows.shape[0] // n
    for place in range(n):
        at = pl.ds(place * padded, share)
        natural[pl.ds(share * (2 * place + l), share)] = own_rows[at].astype(F32)
        natural[pl.ds(share * (2 * place + 1 - l), share)] = other_rows[at].astype(F32)
    out[0] = natural[...].T.astype(BF16)


def per_device(anc_rows, row_home, block_lists, front_blocks, panel, pivot_inverse):
    groups, pan = lax.axis_size("grp"), lax.axis_size("pan")
    n, pairs = pan // 2, groups // 2
    rows, width = panel.shape[1:]
    share = width // pan
    padded = -(-share // 16) * 16
    half = n * padded
    wanted = block_lists.shape[1] // groups * BLK
    windows = pan // groups
    diagonal = (lax.axis_index("grp") ^ lax.axis_index("pan")) & 1 == 0
    inverse = pivot_inverse[0]
    shape = jax.ShapeDtypeStruct

    def at(h, c, q, l):
        return (2 * h + c) * pan + 2 * q + l

    places = [
        (h, c, q, l) for h in range(pairs) for c in range(2) for q in range(n) for l in range(2)
    ]
    exchange = [(at(h, c, q, l), at(h, l, q, c)) for h, c, q, l in places]
    crossing = [(a, b) for a, b in exchange if a != b]
    to_sibling = [(at(h, c, q, l), at(h, 1 - c, q, l)) for h, c, q, l in places if c == l]
    to_diagonal = [(at(h, c, q, l), at(h, c, q, c)) for h, c, q, l in places if c != l]
    cores = [(g, g ^ 1) for g in range(groups)]
    ring = [
        (2 * ring_place(i, n) + l, 2 * ring_place((i + 1) % n, n) + l)
        for i in range(n)
        for l in range(2)
    ]

    def swap(x, name):
        with jax.named_scope(name):
            return lax.ppermute(x, "grp", cores)

    def everywhere(x, pairs_of, name):
        with jax.named_scope(name):
            return lax.ppermute(x, ("grp", "pan"), pairs_of)

    def along(x, pairs_of, name):
        with jax.named_scope(name):
            return lax.ppermute(x, "pan", pairs_of)

    keep, give = pl.pallas_call(
        functools.partial(scale_kernel, pan),
        out_shape=[shape((half, rows), BF16)] * 2,
        in_specs=[HBM] * 3,
        out_specs=[VMEM] * 2,
        scratch_shapes=[
            pltpu.VMEM((rows, width), BF16),
            pltpu.VMEM((width, width), BF16),
            pltpu.VMEM((width, rows), F32),
            pltpu.SMEM(front_blocks.shape, jnp.int32),
            pltpu.SemaphoreType.DMA((3,)),
        ],
        compiler_params=params(60),
        name="scale",
    )(front_blocks, panel[0], inverse)
    given = everywhere(give, to_sibling, "near_half")
    near = jnp.where(diagonal, keep, given)
    far = jnp.where(
        diagonal,
        everywhere(keep, to_diagonal, "far_half"),
        everywhere(give, crossing, "far_half_off"),
    )

    *packed, slots = pl.pallas_call(
        functools.partial(pack_kernel, groups, pan),
        out_shape=[shape((2 * wanted, rows), BF16)] * pairs + [shape((pan,), jnp.int32)],
        in_specs=[HBM, HBM, VMEM, VMEM],
        out_specs=[VMEM] * pairs + [SMEM],
        scratch_shapes=[
            pltpu.SMEM(row_home.shape, jnp.int32),
            pltpu.SMEM(block_lists.shape, jnp.int32),
            pltpu.SMEM((pan,), jnp.int32),
            pltpu.SemaphoreType.DMA((2,)),
        ],
        compiler_params=params(),
        name="pack",
    )(row_home, block_lists, anc_rows, swap(anc_rows, "rows_of_sibling"))
    own_columns = lax.dynamic_slice_in_dim(inverse, lax.axis_index("pan") * share, share, 1)
    triangle = lax.dot_general(
        own_columns, inverse, (((0,), (0,)), ((), ())), preferred_element_type=F32
    )

    nears, fars = [near], [far]
    for step in range(1, n):
        nears.append(along(nears[-1], ring, f"near_{step}"))
        fars.append(along(fars[-1], ring, f"far_{step}"))

    whole = jnp.zeros((pan, half, rows), BF16)
    anywhere = pl.BlockSpec(memory_space=pl.ANY)
    for k in range(n):
        for side, chunks in enumerate((nears, fars)):
            whole = pl.pallas_call(
                functools.partial(place_kernel, n, k, side),
                out_shape=shape((pan, half, rows), BF16),
                in_specs=[anywhere, anywhere],
                out_specs=anywhere,
                scratch_shapes=[pltpu.SemaphoreType.DMA(())],
                input_output_aliases={1: 0},
                cost_estimate=pl.CostEstimate(flops=PLACE, bytes_accessed=0, transcendentals=0),
                compiler_params=params(),
                name="place",
            )(chunks[k], whole)
    arrived = [
        everywhere(
            packed[k],
            [(at(h, c, q, l), at(peer(h, k, pairs), l, q, c)) for h, c, q, l in places],
            f"sigma_{k}",
        )
        for k in range(pairs)
    ]
    swapped = [swap(piece, f"share_{k}") for k, piece in enumerate(arrived)]
    triangle, _ = lax.optimization_barrier((triangle, nears[-2]))
    own_sigma, other_sigma = pl.pallas_call(
        functools.partial(stack_kernel, pairs),
        out_shape=[shape((pan, wanted // windows, rows), BF16)] * 2,
        in_specs=[VMEM] * groups,
        out_specs=[VMEM] * 2,
        compiler_params=params(),
        cost_estimate=pl.CostEstimate(flops=STACK, bytes_accessed=0, transcendentals=0),
        name="stack",
    )(*arrived, *swapped)
    mine, give, *parts = pl.pallas_call(
        functools.partial(cross_kernel, n),
        out_shape=[shape((half, rows), BF16)] * 2
        + [shape((padded, 2 * rows), BF16)] * n,
        in_specs=[SMEM] * 2 + [VMEM] * 3,
        out_specs=[VMEM] * (n + 2),
        scratch_shapes=[pltpu.VMEM((2, half, rows), F32)],
        compiler_params=params(),
        name="cross",
    )(front_blocks, slots, whole, own_sigma, other_sigma)

    for k in range(1, n):
        parts[k] = along(
            parts[k],
            [(2 * q + l, 2 * peer(q, k, n) + l) for q in range(n) for l in range(2)],
            f"columns_{k}",
        )
    other_whole = swap(whole, "scaled_of_sibling")
    own_rows = everywhere(mine, exchange, "rows_out")
    other_rows = everywhere(
        give, [(at(h, c, q, l), at(h, l, q, 1 - c)) for h, c, q, l in places], "rows_out_other"
    )
    firsts = pl.pallas_call(
        functools.partial(pivot_first_kernel, n),
        out_shape=[shape((padded, half), F32)] * 2,
        in_specs=[VMEM] * 3,
        out_specs=[VMEM] * 2,
        compiler_params=params(),
        name="pivot_first",
    )(parts[0], whole, other_whole)
    term = pl.pallas_call(
        functools.partial(pivot_kernel, n, share),
        out_shape=shape((padded, width), BF16),
        in_specs=[VMEM] * (n + 3),
        out_specs=VMEM,
        compiler_params=params(),
        name="pivot",
    )(*firsts, *parts[1:], whole, other_whole)
    term = everywhere(term, exchange, "term_out")
    cross = pl.pallas_call(
        functools.partial(turn_kernel, pan, share),
        out_shape=shape((1, rows, width), BF16),
        in_specs=[VMEM, VMEM],
        out_specs=VMEM,
        scratch_shapes=[pltpu.VMEM((width, rows), F32)],
        compiler_params=params(),
        name="turn",
    )(own_rows, other_rows)
    pivot = triangle + term[:share].astype(F32)
    return cross, pivot[None]


def solution(mesh):
    placed = (P("grp", "pan"), P(), P(), P(), P("grp", "pan", None), P("grp", None, None))
    return jax.shard_map(
        per_device,
        mesh=mesh,
        in_specs=placed,
        out_specs=(P("grp", "pan", None), P("grp", "pan", None)),
        check_vma=False,
    )
```

```python
import functools

import jax
import jax.numpy as jnp
from jax import lax
from jax.experimental import pallas as pl
from jax.experimental.pallas import tpu as pltpu
from jax.sharding import PartitionSpec as P

BLK = 128
PLACE = 1_000_000_000
STACK = 12_000_000_000
F32 = jnp.float32
BF16 = jnp.bfloat16

VMEM = pl.BlockSpec(memory_space=pltpu.VMEM)
SMEM = pl.BlockSpec(memory_space=pltpu.SMEM)
HBM = pl.BlockSpec(memory_space=pltpu.HBM)


def power_of_two(n):
    return n & (n - 1) == 0


def peer(q, k, n):
    return q ^ k if power_of_two(n) else (q + k) % n


def source(q, k, n):
    return q ^ k if power_of_two(n) else (q + n - k) % n


def ring_place(position, n):
    return position ^ (position >> 1) if power_of_two(n) else position


def ring_position(place, n):
    position = place
    if power_of_two(n):
        shift = 1
        while shift < n:
            position = position ^ (place >> shift)
            shift += 1
    return position


def far_first(n):
    return [0, *range(2, n), *range(1, min(n, 2))]


def coordinates():
    g, p = lax.axis_index("grp"), lax.axis_index("pan")
    return g >> 1, g & 1, p >> 1, p & 1


def params(mib=16):
    return pltpu.CompilerParams(vmem_limit_bytes=mib * 1024 * 1024)


def pack_kernel(groups, pan, row_home_in, lists_in, anc, other_anc, *rest):
    pairs = groups // 2
    outs, members = rest[:pairs], rest[pairs]
    row_home, lists, place, sems = rest[pairs + 1 :]
    loads = [
        pltpu.make_async_copy(row_home_in, row_home, sems.at[0]),
        pltpu.make_async_copy(lists_in, lists, sems.at[1]),
    ]
    for load in loads:
        load.start()
    for load in loads:
        load.wait()
    h, c, q, l = coordinates()
    p = 2 * q + l
    stored = anc.shape[0] // BLK
    window_blocks = anc.shape[1] // BLK
    picked = lists.shape[1] // pan
    windows = pan // groups

    owners = [row_home[window_blocks * w] // stored for w in range(pan)]
    for w in range(pan):
        rank = jnp.int32(0)
        for v in range(w):
            rank = rank + (owners[v] == owners[w]).astype(jnp.int32)
        step = owners[w] >> 1
        step = step ^ h if power_of_two(pairs) else (h + pairs - step) % pairs
        members[(2 * step + (owners[w] & 1)) * windows + rank] = jnp.int32(w)

        @pl.when(owners[w] >> 1 == h)
        def _():
            place[(owners[w] & 1) * windows + rank] = jnp.int32(w)

    for k in range(pairs):
        front = 2 * peer(h, k, pairs) + c
        columns = [lists[front, picked * p + s] - window_blocks * p for s in range(picked)]
        for core in range(2):
            for rank in range(windows):
                w = place[core * windows + rank]
                for r in range(picked):
                    row = row_home[lists[front, picked * w + r]] - stored * (2 * h + core)
                    rows = pl.ds(pl.multiple_of(row * BLK, BLK), BLK)
                    for s in range(picked):
                        at = pl.ds(pl.multiple_of(columns[s] * BLK, BLK), BLK)
                        to = pl.ds(((core * windows + rank) * picked + r) * BLK, BLK)
                        outs[k][to, pl.ds(s * BLK, BLK)] = jnp.where(c == core, anc[rows, at], other_anc[rows, at])


def scale_kernel(
    pan, front_blocks_in, panel_in, inverse_in, keep, give, panel, inverse, turned, front_blocks, sems
):
    h, c, q, l = coordinates()
    g, p = 2 * h + c, 2 * q + l
    loads = [
        pltpu.make_async_copy(inverse_in, inverse, sems.at[0]),
        pltpu.make_async_copy(panel_in, panel, sems.at[1]),
        pltpu.make_async_copy(front_blocks_in, front_blocks, sems.at[2]),
    ]
    for load in loads:
        load.start()
    for load in loads:
        load.wait()
    rows, width = panel.shape
    n, share = pan // 2, width // pan
    padded = keep.shape[0] // n
    live = front_blocks[g]
    scaled = jnp.dot(panel[...], inverse[...], preferred_element_type=F32)
    row = lax.broadcasted_iota(jnp.int32, scaled.shape, 0)
    scaled = jnp.where(p * (rows // BLK) + row // BLK < live, scaled, 0.0)
    turned[...] = scaled.T
    if padded != share:
        keep[...] = jnp.zeros_like(keep)
        give[...] = jnp.zeros_like(give)
    for place in range(n):
        at = pl.ds(place * padded, share)
        keep[at] = turned[pl.ds(share * (2 * place + c), share)].astype(BF16)
        give[at] = turned[pl.ds(share * (2 * place + 1 - c), share)].astype(BF16)


def stack_kernel(pairs, members, *refs):
    own_in, other_in, out = refs[:pairs], refs[pairs : 2 * pairs], refs[2 * pairs]
    _, c, _, _ = coordinates()
    count = members.shape[0]
    depth, rows = out.shape[0] // count, out.shape[1] // 2
    windows = count // pairs
    for slot in range(count):
        at = pl.ds(slot % windows * depth, depth)
        to = pl.ds(pl.multiple_of(members[slot] * depth, depth), depth)
        own, other = own_in[slot // windows][at], other_in[slot // windows][at]
        out[to, :rows] = jnp.where(c == 0, own, other)
        out[to, rows:] = jnp.where(c == 0, other, own)


def place_kernel(n, k, side, chunk, _, whole, sem):
    _, _, q, l = coordinates()
    origin = ring_place((ring_position(q, n) + n - k) % n, n)
    rows = chunk.shape[1]
    at = pl.ds(pl.multiple_of((2 * origin + (l ^ side)) * rows, rows), rows)
    copy = pltpu.make_async_copy(chunk, whole.at[:, at], sem)
    copy.start()
    copy.wait()


def cross_kernel(n, front_blocks, whole, sigma, mine, give, *rest):
    parts, total = rest[:n], rest[n]
    h, c, q, l = coordinates()
    half, rows = mine.shape
    padded = half // n
    product = jnp.dot(whole[...], sigma[...], preferred_element_type=F32)
    block = (2 * q * rows + lax.broadcasted_iota(jnp.int32, product.shape, 1)) // BLK
    product = jnp.where(block < front_blocks[2 * h + l], -product, 0.0)
    total[...] = product
    product = product.astype(BF16)
    mine[...] = jnp.where(c == 0, product[:, :rows], product[:, rows:])
    give[...] = jnp.where(c == 0, product[:, rows:], product[:, :rows])
    for k in range(n):
        at = pl.ds(pl.multiple_of(peer(q, k, n) * padded, padded), padded)
        parts[k][...] = total[at].astype(BF16)


def pivot_kernel(n, share, *rest):
    parts, (own_scaled, other_scaled, out, columns) = rest[:n], rest[n:]
    _, c, q, _ = coordinates()
    padded, depth = parts[0].shape
    for k, part in zip(far_first(n), parts):
        at = pl.ds(pl.multiple_of(source(q, k, n) * depth, depth), depth)
        columns[:, at] = part[...]
    across = (((1,), (1,)), ((), ()))
    own, other = [
        lax.dot_general(columns[...], scaled[...], across, preferred_element_type=F32)
        for scaled in (own_scaled, other_scaled)
    ]
    low = jnp.where(c == 0, own, other)
    high = jnp.where(c == 0, other, own)
    pieces = []
    for place in range(n):
        at = slice(place * padded, place * padded + share)
        pieces += [low[:, at], high[:, at]]
    out[...] = (-jnp.concatenate(pieces, axis=1)).astype(BF16)


def turn_kernel(pan, share, own_rows, other_rows, out, natural):
    _, _, _, l = coordinates()
    n = pan // 2
    padded = own_rows.shape[0] // n
    for place in range(n):
        at = pl.ds(place * padded, share)
        natural[pl.ds(share * (2 * place + l), share)] = own_rows[at].astype(F32)
        natural[pl.ds(share * (2 * place + 1 - l), share)] = other_rows[at].astype(F32)
    out[0] = natural[...].T.astype(BF16)


def per_device(anc_rows, row_home, block_lists, front_blocks, panel, pivot_inverse):
    groups, pan = lax.axis_size("grp"), lax.axis_size("pan")
    n, pairs = pan // 2, groups // 2
    rows, width = panel.shape[1:]
    share = width // pan
    padded = -(-share // 16) * 16
    half = n * padded
    wanted = block_lists.shape[1] // groups * BLK
    windows = pan // groups
    diagonal = (lax.axis_index("grp") ^ lax.axis_index("pan")) & 1 == 0
    inverse = pivot_inverse[0]
    shape = jax.ShapeDtypeStruct

    def at(h, c, q, l):
        return (2 * h + c) * pan + 2 * q + l

    places = [
        (h, c, q, l) for h in range(pairs) for c in range(2) for q in range(n) for l in range(2)
    ]
    exchange = [(at(h, c, q, l), at(h, l, q, c)) for h, c, q, l in places]
    crossing = [(a, b) for a, b in exchange if a != b]
    to_sibling = [(at(h, c, q, l), at(h, 1 - c, q, l)) for h, c, q, l in places if c == l]
    to_diagonal = [(at(h, c, q, l), at(h, c, q, c)) for h, c, q, l in places if c != l]
    cores = [(g, g ^ 1) for g in range(groups)]
    ring = [
        (2 * ring_place(i, n) + l, 2 * ring_place((i + 1) % n, n) + l)
        for i in range(n)
        for l in range(2)
    ]

    def swap(x, name):
        with jax.named_scope(name):
            return lax.ppermute(x, "grp", cores)

    def everywhere(x, pairs_of, name):
        with jax.named_scope(name):
            return lax.ppermute(x, ("grp", "pan"), pairs_of)

    def along(x, pairs_of, name):
        with jax.named_scope(name):
            return lax.ppermute(x, "pan", pairs_of)

    keep, give = pl.pallas_call(
        functools.partial(scale_kernel, pan),
        out_shape=[shape((half, rows), BF16)] * 2,
        in_specs=[HBM] * 3,
        out_specs=[VMEM] * 2,
        scratch_shapes=[
            pltpu.VMEM((rows, width), BF16),
            pltpu.VMEM((width, width), BF16),
            pltpu.VMEM((width, rows), F32),
            pltpu.SMEM(front_blocks.shape, jnp.int32),
            pltpu.SemaphoreType.DMA((3,)),
        ],
        compiler_params=params(60),
        name="scale",
    )(front_blocks, panel[0], inverse)
    given = everywhere(give, to_sibling, "near_half")
    near = jnp.where(diagonal, keep, given)
    far = jnp.where(
        diagonal,
        everywhere(keep, to_diagonal, "far_half"),
        everywhere(give, crossing, "far_half_off"),
    )

    *packed, members = pl.pallas_call(
        functools.partial(pack_kernel, groups, pan),
        out_shape=[shape((2 * wanted, rows), BF16)] * pairs + [shape((pan,), jnp.int32)],
        in_specs=[HBM, HBM, VMEM, VMEM],
        out_specs=[VMEM] * pairs + [SMEM],
        scratch_shapes=[
            pltpu.SMEM(row_home.shape, jnp.int32),
            pltpu.SMEM(block_lists.shape, jnp.int32),
            pltpu.SMEM((pan,), jnp.int32),
            pltpu.SemaphoreType.DMA((2,)),
        ],
        compiler_params=params(),
        name="pack",
    )(row_home, block_lists, anc_rows, swap(anc_rows, "rows_of_sibling"))
    own_columns = lax.dynamic_slice_in_dim(inverse, lax.axis_index("pan") * share, share, 1)
    triangle = lax.dot_general(
        own_columns, inverse, (((0,), (0,)), ((), ())), preferred_element_type=F32
    )

    nears, fars = [near], [far]
    for step in range(1, n):
        nears.append(along(nears[-1], ring, f"near_{step}"))
        fars.append(along(fars[-1], ring, f"far_{step}"))

    whole = jnp.zeros((half, pan * rows), BF16)
    anywhere = pl.BlockSpec(memory_space=pl.ANY)
    for k in range(n):
        for side, chunks in enumerate((nears, fars)):
            whole = pl.pallas_call(
                functools.partial(place_kernel, n, k, side),
                out_shape=shape(whole.shape, BF16),
                in_specs=[anywhere, anywhere],
                out_specs=anywhere,
                scratch_shapes=[pltpu.SemaphoreType.DMA(())],
                input_output_aliases={1: 0},
                cost_estimate=pl.CostEstimate(flops=PLACE, bytes_accessed=0, transcendentals=0),
                compiler_params=params(),
                name="place",
            )(chunks[k], whole)
    arrived = [
        everywhere(
            packed[k],
            [(at(h, c, q, l), at(peer(h, k, pairs), l, q, c)) for h, c, q, l in places],
            f"sigma_{k}",
        )
        for k in range(pairs)
    ]
    swapped = [swap(piece, f"share_{k}") for k, piece in enumerate(arrived)]
    triangle, _ = lax.optimization_barrier((triangle, nears[-2]))
    sigma = pl.pallas_call(
        functools.partial(stack_kernel, pairs),
        out_shape=shape((pan * wanted // windows, 2 * rows), BF16),
        in_specs=[SMEM] + [VMEM] * groups,
        out_specs=VMEM,
        compiler_params=params(),
        cost_estimate=pl.CostEstimate(flops=STACK, bytes_accessed=0, transcendentals=0),
        name="stack",
    )(members, *arrived, *swapped)
    mine, give, *parts = pl.pallas_call(
        functools.partial(cross_kernel, n),
        out_shape=[shape((half, rows), BF16)] * 2
        + [shape((padded, 2 * rows), BF16)] * n,
        in_specs=[SMEM] + [VMEM] * 2,
        out_specs=[VMEM] * (n + 2),
        scratch_shapes=[pltpu.VMEM((half, 2 * rows), F32)],
        compiler_params=params(),
        name="cross",
    )(front_blocks, whole, sigma)

    for k in far_first(n)[1:]:
        parts[k] = along(
            parts[k],
            [(2 * q + l, 2 * peer(q, k, n) + l) for q in range(n) for l in range(2)],
            f"columns_{k}",
        )
    other_whole = swap(whole, "scaled_of_sibling")
    own_rows = everywhere(mine, exchange, "rows_out")
    other_rows = everywhere(
        give, [(at(h, c, q, l), at(h, l, q, 1 - c)) for h, c, q, l in places], "rows_out_other"
    )
    term = pl.pallas_call(
        functools.partial(pivot_kernel, n, share),
        out_shape=shape((padded, width), BF16),
        in_specs=[VMEM] * (n + 2),
        out_specs=VMEM,
        scratch_shapes=[pltpu.VMEM((padded, pan * rows), BF16)],
        compiler_params=params(),
        name="pivot",
    )(*[parts[k] for k in far_first(n)], whole, other_whole)
    term = everywhere(term, exchange, "term_out")
    cross = pl.pallas_call(
        functools.partial(turn_kernel, pan, share),
        out_shape=shape((1, rows, width), BF16),
        in_specs=[VMEM, VMEM],
        out_specs=VMEM,
        scratch_shapes=[pltpu.VMEM((width, rows), F32)],
        compiler_params=params(),
        name="turn",
    )(own_rows, other_rows)
    pivot = triangle + term[:share].astype(F32)
    return cross, pivot[None]


def solution(mesh):
    placed = (P("grp", "pan"), P(), P(), P(), P("grp", "pan", None), P("grp", None, None))
    return jax.shard_map(
        per_device,
        mesh=mesh,
        in_specs=placed,
        out_specs=(P("grp", "pan", None), P("grp", "pan", None)),
        check_vma=False,
    )
```
